1024 devices in a mesh: hst: 64 (over z, core), dev: 16 (over x, y).
Axes of the slice: x: 4, y: 4, z: 32, core: 2. Of those that a mesh axis runs over, the one named last changes fastest.
Arguments:
- cache_table: bfloat16 [1024, 512], P('dev'), may hold values from -6 to 6
- cold_table: bfloat16 [262144, 512], P(('hst', 'dev')), may hold values from -6 to 6
- hit_ids: int32 [16384, 32], P(('hst', 'dev')), may hold values from 0 to 63
- miss_owner: int32 [262144, 1], P(('hst', 'dev')), may hold values from 0 to 63; in each aligned block of 256 rows (0 to 255, 256 to 511, ...) at most 8 rows name the same one
- miss_row: int32 [262144], P(('hst', 'dev')), may hold values from 0 to 255
- history_ids: int32 [2048, 512], P(('hst', 'dev')), may hold values from 0 to 767
- candidate_ids: int32 [2048, 128], P(('hst', 'dev')), may hold values from 0 to 767
- history_len: int32 [2048], P(('hst', 'dev')), may hold values from 64 to 512
- w_kv: bfloat16 [512, 1024], replicated, may hold values from -0.25 to 0.25
- w_cand: bfloat16 [512, 2048], replicated, may hold values from -0.25 to 0.25
- w_out: bfloat16 [512, 512], replicated, may hold values from -0.25 to 0.25
- w_score: float32 [512], replicated, may hold values from -0.25 to 0.25
Outputs:
- scores: float32 [2048, 128], P(('hst', 'dev'))
The draws below stay inside these ranges and needn't reach their ends.
Inputs may be any that keep to these rules, and one draw needn't show every extreme that they name: `hit_ids`: each id names a row of the cache shard held by the device of the asker's host group whose index along dev is the id's row number modulo the size of dev. `miss_owner`: a missed row lies in the cold shard of the owner group's device that has the asker's index along dev; each device names one group at most 8 times.
All inputs are finite; a program needn't handle non-finite values.
Results may differ from the reference program's by a relative error of at most 0.0039.
Values may be sent and summed in bfloat16 or wider, within the bound.
A program may use at most 32 MiB of HBM per device.

```python
import math
import jax
import jax.numpy as jnp
import numpy as np
from jax import lax

D = 512
HEADS = 4
DH = 128
CACHE_DEV = 64
COLD_DEV = 256
HIT_SLOTS = 32
MISS_CAP = 8
MISS_DEV = 256
FETCHED = 768
USER_DEV = 2
HIST = 512
CANDS = 128
USERS = 2048
N_HST = 64
N_DEV = 16
DEVICES = 1024


def draw_history_len(key, part):
    key = jax.random.fold_in(key, 5)
    first, second = jax.random.split(key, 2)
    lengths = jax.random.randint(first, (USERS,), HIST // 8, HIST + 1, dtype=jnp.int32)
    places = jax.random.permutation(second, USERS)
    position = jnp.arange(USERS, dtype=jnp.int32)
    lengths = jnp.where(position == places[0], HIST, lengths)
    lengths = jnp.where(position == places[-1], HIST // 8, lengths)
    return lengths.astype(jnp.int32)


def with_ends(array, key, low, top_value):
    place = [jax.random.randint(jax.random.fold_in(key, axis), (), 0, length) for axis, length in enumerate(array.shape)]
    main_axis = array.shape.index(max(array.shape))
    beside = place[:main_axis] + [(place[main_axis] + 1) % array.shape[main_axis]] + place[main_axis + 1:]
    return array.at[tuple(place)].set(low).at[tuple(beside)].set(top_value)


def shard_levels(rng, extent, shards, smallest, top_value):
    level, own = 1.0, jax.random.fold_in(rng, 6)
    for axis_at, parts in shards:
        heights = jnp.exp(jax.random.uniform(jax.random.fold_in(own, axis_at), (parts,), jnp.float32, smallest / len(shards), top_value / len(shards)))
        level = level * jnp.repeat(heights, extent[axis_at] // parts).reshape([-1 if axis == axis_at else 1 for axis in range(len(extent))])
    return level


def assign_block(own_key, own, number, rows, amount, top, most, lean):
    sequence = jax.random.permutation(own_key, amount)
    packed, ordinary = portions_of(amount, rows * top, most, lean, True), portions_of(amount, rows * top, most, lean, False)
    places = jnp.arange(amount)

    def named(sizes, turn):
        used = int((sizes > 0).sum())
        fixed = max(1, used // 4)
        shifted = fixed + (places - fixed + turn * (used - fixed)) % max(1, amount - fixed)
        return jnp.zeros((amount,), jnp.int32).at[sequence[jnp.where(places < fixed, places, shifted)]].set(jnp.asarray(sizes, jnp.int32))

    sizes = jnp.where(number % 4 == 0, named(packed, number // 4), named(ordinary, number - number // 4 - 1))
    mixed = jax.random.permutation(jax.random.fold_in(own, 3), amount)
    donor, sink = mixed[0:amount // 2 * 2:2], mixed[1:amount // 2 * 2:2]
    margin = jnp.minimum(sizes[donor] - 1, most - sizes[sink]) // 2
    margin = jnp.where((donor == sequence[0]) | (sink == sequence[0]) | (sizes[sink] == 0), 0, jnp.maximum(margin, 0))
    shifted = jax.random.randint(jax.random.fold_in(own, 4), (amount // 2,), 0, 1 << 20) % (margin + 1)
    sizes = sizes.at[donor].add(-shifted).at[sink].add(shifted)
    labels = jnp.searchsorted(jnp.cumsum(sizes), jnp.arange(rows * top), side="right").astype(jnp.int32)
    grid = labels.reshape(top, rows).T
    grid = grid[jax.random.permutation(jax.random.fold_in(own, 1), rows)]
    turn = jax.random.randint(jax.random.fold_in(own, 2), (rows, 1), 0, top)
    return jnp.take_along_axis(grid, (jnp.arange(top)[None, :] + turn) % top, axis=1)


def portions_of(number_of, total, bound, skew, full):
    loads = [(1 << 20) // math.isqrt(grade ** skew) + 1 for grade in range(1, number_of + 1)]
    largest = bound if full else min(bound, max(-(-total // number_of), total * loads[0] // sum(loads)))
    least = 1 if total - largest >= number_of - 1 else 0
    given, surplus = [largest] + [least] * (number_of - 1), total - largest - least * (number_of - 1)
    while surplus > 0:
        free = [i for i in range(1, number_of) if given[i] < largest] or [i for i in range(1, number_of) if given[i] < bound]
        mass, remaining = sum([loads[i] for i in free]), surplus
        for i in free:
            more = min(bound - given[i], max(1, remaining * loads[i] // mass), surplus)
            given[i] = given[i] + more
            surplus = surplus - more
    return np.array(given)


def centred(own_key, shape, deviation, most, cuts=(), kind=jnp.bfloat16):
    gain = shard_levels(own_key, shape, cuts, -0.22, 0.18) if cuts else 1.0
    entries = jax.random.normal(own_key, shape, jnp.float32) * deviation * gain
    return jnp.minimum(jnp.maximum(entries, -most), most).astype(kind)


def setup_inputs(seed: int = 0) -> dict:
    key_list = jax.random.split(jax.random.key(seed), 13)
    cache_table = centred(key_list[0], (CACHE_DEV * N_DEV, D), 1.0, 6.0, ((0, 16),))
    cold_table = centred(key_list[1], (COLD_DEV * DEVICES, D), 1.0, 6.0, ((0, 1024),))
    hit_ids = with_ends(jax.random.randint(key_list[2], (DEVICES * N_DEV, HIT_SLOTS), 0, CACHE_DEV), jax.random.fold_in(key_list[2], 1), 0, CACHE_DEV - 1).astype(jnp.int32)
    miss_owner_keys = jax.random.split(jax.random.fold_in(key_list[3], 1), (DEVICES * MISS_DEV) // MISS_DEV)
    miss_owner_turns = jax.random.permutation(jax.random.fold_in(key_list[3], 3), (DEVICES * MISS_DEV) // MISS_DEV)
    miss_owner = jax.vmap(lambda own, number: assign_block(jax.random.fold_in(key_list[3], 2), own, number, MISS_DEV, N_HST, 1, MISS_CAP, 2))(miss_owner_keys, miss_owner_turns).reshape((DEVICES * MISS_DEV, 1))
    miss_row = with_ends(jax.random.randint(key_list[4], (DEVICES * MISS_DEV,), 0, COLD_DEV), jax.random.fold_in(key_list[4], 1), 0, COLD_DEV - 1).astype(jnp.int32)
    history_ids = with_ends(jax.random.randint(key_list[5], (USERS, HIST), 0, FETCHED), jax.random.fold_in(key_list[5], 1), 0, FETCHED - 1).astype(jnp.int32)
    candidate_ids = with_ends(jax.random.randint(key_list[6], (USERS, CANDS), 0, FETCHED), jax.random.fold_in(key_list[6], 1), 0, FETCHED - 1).astype(jnp.int32)
    history_len = draw_history_len(jax.random.fold_in(key_list[12], 71), 0)
    w_kv = centred(key_list[8], (D, 2 * D), D ** -0.5, 0.25)
    w_cand = centred(key_list[9], (D, 4 * D), D ** -0.5, 0.25)
    w_out = centred(key_list[10], (D, D), D ** -0.5, 0.25)
    w_score = centred(key_list[11], (D,), D ** -0.5, 0.25, (), jnp.float32)
    return {"cache_table": cache_table, "cold_table": cold_table, "hit_ids": hit_ids, "miss_owner": miss_owner, "miss_row": miss_row, "history_ids": history_ids, "candidate_ids": candidate_ids, "history_len": history_len, "w_kv": w_kv, "w_cand": w_cand, "w_out": w_out, "w_score": w_score}


def normalize(values):
    mean = lax.optimization_barrier(jnp.mean(values, axis=-1, keepdims=True))
    centered = values - mean
    var = lax.optimization_barrier(jnp.mean(centered * centered, axis=-1, keepdims=True))
    return centered / jnp.sqrt(var + 1e-05)

def layer(collected, hist_rows, cand_rows, lengths, w_kv, w_cand, w_out, w_score):
    history_x = jnp.take(collected, hist_rows, axis=0)
    cand_x = jnp.take(collected, cand_rows, axis=0)
    history_n = normalize(history_x.astype(jnp.float32)).astype(jnp.bfloat16)
    cand_n = normalize(cand_x.astype(jnp.float32)).astype(jnp.bfloat16)
    kv = jax.nn.silu(jnp.einsum('uld,de->ule', history_n.astype(jnp.float32), w_kv.astype(jnp.float32))).astype(jnp.bfloat16)
    proj = jax.nn.silu(jnp.einsum('ucd,de->uce', cand_n.astype(jnp.float32), w_cand.astype(jnp.float32))).astype(jnp.bfloat16)
    users, hist = hist_rows.shape
    cands = cand_rows.shape[1]
    keys = kv[..., :D].reshape(users, hist, HEADS, DH)
    values = kv[..., D:].reshape(users, hist, HEADS, DH)
    gate = proj[..., :D]
    cand_value = proj[..., D:2 * D].reshape(users, cands, HEADS, DH)
    query = proj[..., 2 * D:3 * D].reshape(users, cands, HEADS, DH)
    cand_key = proj[..., 3 * D:].reshape(users, cands, HEADS, DH)
    scale = 1.0 / math.sqrt(DH)
    live = (jnp.arange(hist, dtype=jnp.int32)[None, :] < lengths[:, None]).astype(jnp.float32)
    raw = jnp.einsum('uchd,ulhd->uhcl', query.astype(jnp.float32), keys.astype(jnp.float32)) * scale
    weight = (jax.nn.silu(raw) * live[:, None, None, :]).astype(jnp.bfloat16)
    summed = jnp.einsum('uhcl,ulhd->uchd', weight.astype(jnp.float32), values.astype(jnp.float32))
    own = lax.optimization_barrier(jnp.sum(query.astype(jnp.float32) * cand_key.astype(jnp.float32), axis=-1)) * scale
    attended = summed / lengths.astype(jnp.float32)[:, None, None, None] + jax.nn.silu(own)[..., None] * cand_value.astype(jnp.float32)
    attended = attended.reshape(users, cands, D)
    mixed = (normalize(attended) * gate.astype(jnp.float32)).astype(jnp.bfloat16)
    branch = jnp.dot(mixed.reshape(users * cands, D), w_out, preferred_element_type=jnp.float32).reshape(users, cands, D)
    output = cand_x.astype(jnp.float32) + branch
    return lax.optimization_barrier(jnp.sum(output * w_score, axis=-1))

def reference(cache_table, cold_table, hit_ids, miss_owner, miss_row, history_ids, candidate_ids, history_len, w_kv, w_cand, w_out, w_score):
    anchor = jnp.zeros((), jnp.int32)

    def one_device(rank):
        rank = rank.astype(jnp.int32)
        lane = rank % N_DEV
        asked = lax.dynamic_slice(hit_ids, ((rank * N_DEV).astype(jnp.int32), anchor), (N_DEV, HIT_SLOTS))
        peers = jnp.arange(N_DEV, dtype=jnp.int32)[:, None] * CACHE_DEV
        hit_rows = jnp.take(cache_table, (peers + asked).reshape(-1), axis=0)
        miss_start = (rank * MISS_DEV).astype(jnp.int32)
        owners = lax.dynamic_slice(miss_owner, (miss_start, anchor), (MISS_DEV, 1))[:, 0]
        within = lax.dynamic_slice(miss_row, (miss_start,), (MISS_DEV,))
        miss_rows = jnp.take(cold_table, ((owners * N_DEV + lane) * COLD_DEV + within).astype(jnp.int32), axis=0)
        collected = jnp.concatenate([hit_rows, miss_rows], axis=0)
        user_start = (rank * USER_DEV).astype(jnp.int32)
        hist_rows = lax.dynamic_slice(history_ids, (user_start, anchor), (USER_DEV, HIST))
        cand_rows = lax.dynamic_slice(candidate_ids, (user_start, anchor), (USER_DEV, CANDS))
        lengths = lax.dynamic_slice(history_len, (user_start,), (USER_DEV,))
        return layer(collected, hist_rows, cand_rows, lengths, w_kv, w_cand, w_out, w_score)
    ranks = jnp.arange(DEVICES, dtype=jnp.int32)
    return lax.map(one_device, ranks).reshape(USERS, CANDS)
```

```python
import functools
import math

import jax
import jax.numpy as jnp
from jax import lax
from jax.experimental import pallas as pl
from jax.experimental.pallas import tpu as pltpu
from jax.sharding import PartitionSpec as P

F32 = jnp.float32
BF16 = jnp.bfloat16
HEADS = 4
DH = 128
CAP = 8
EPS = 1e-05


def iota(shape, dim):
    return lax.broadcasted_iota(jnp.int32, shape, dim)


def normalize(x):
    centered = x - jnp.mean(x, axis=-1, keepdims=True)
    var = jnp.mean(centered * centered, axis=-1, keepdims=True)
    return centered * lax.rsqrt(var + EPS)


def silu_of_double(y):
    return y + y * jnp.tanh(y)


def dot(a, b):
    return jnp.dot(a, b, preferred_element_type=F32)


def dot_nt(a, b):
    return lax.dot_general(a, b, (((1,), (1,)), ((), ())), preferred_element_type=F32)


def columns(rows):
    r, n = rows.shape
    eye = iota((n, n), 0) == iota((n, n), 1)
    spread = jnp.where(eye[None], jnp.broadcast_to(rows[:, None, :], (r, n, n)), 0.0)
    return jnp.sum(spread, axis=-1, keepdims=True).reshape(r * n, 1)


def onehot(column, width):
    lanes = iota((column.shape[0], width), 1).astype(F32)
    return jnp.where(column == lanes, 1.0, 0.0).astype(BF16)


def kernel(
    n_hst,
    n_dev,
    cache,
    cold,
    hit_ids,
    owner,
    miss_row,
    history_ids,
    candidate_ids,
    history_len,
    w_kv_hbm,
    w_cand_hbm,
    w_out_hbm,
    w_score,
    out,
    w_kv,
    w_cand,
    w_out,
    asked,
    request,
    reply,
    arrived,
    cached,
    kv,
    w_sem,
    ask_send,
    ask_recv,
    row_send,
    row_recv,
    ag_send,
    ag_recv,
    swap_send,
    swap_recv,
):
    me = lax.axis_index("hst")
    dev = lax.axis_index("dev")
    z, core = me // 2, lax.rem(me, 2)
    nz = n_hst // 2
    far = nz // 2
    hits = hit_ids.shape[0] * hit_ids.shape[1]
    misses = owner.shape[0] * owner.shape[1]
    width = cache.shape[1]
    half_w = width // 2
    half = cache.shape[0] // 2
    chunk = n_hst // row_recv.shape[0]
    chunks = n_hst // chunk

    def group_at(k, sign):
        pair = k // 2
        step = (far - (pair + 1) // 2) * (2 * lax.rem(pair, 2) - 1)
        chip = lax.rem(z + sign * step + nz, nz)
        return chip * 2 + lax.rem(core + 1 - lax.rem(k, 2), 2)

    weights = [
        pltpu.make_async_copy(w_kv_hbm, w_kv, w_sem.at[0]),
        pltpu.make_async_copy(w_cand_hbm, w_cand, w_sem.at[1]),
        pltpu.make_async_copy(w_out_hbm, w_out, w_sem.at[2]),
    ]

    barrier = pltpu.get_barrier_semaphore()

    def greet_group(k, carry):
        pl.semaphore_signal(barrier, inc=1, device_id={"hst": group_at(k, 1), "dev": dev})
        return carry

    def greet_dev(k, carry):
        pl.semaphore_signal(barrier, inc=1, device_id={"hst": me, "dev": lax.rem(dev + k, n_dev)})
        return carry

    lax.fori_loop(0, n_hst - 1, greet_group, 0)
    lax.fori_loop(1, n_dev, greet_dev, 0)
    for w in weights:
        w.start()

    owners = owner[...].astype(F32)
    owner_col = columns(owners)
    row_col = columns(miss_row[...].astype(F32))
    by_miss = onehot(owner_col, 128)
    earlier = jnp.where(iota((misses, misses), 1) < iota((misses, misses), 0), 1.0, 0.0).astype(BF16)
    before = dot(earlier, by_miss)
    slot_col = jnp.sum(before * by_miss.astype(F32), axis=-1, keepdims=True)
    lanes = iota((misses, 128), 1).astype(F32)
    rows_at_slot = jnp.where(slot_col == lanes, row_col, 0.0).astype(BF16)
    wanted = jnp.zeros((n_hst, 128), F32)
    groups = iota((n_hst, 128), 0).astype(F32)
    for i in range(misses // 128):
        by_group = jnp.where(owners[i : i + 1] == groups, 1.0, 0.0).astype(BF16)
        wanted = wanted + dot(by_group, rows_at_slot[i * 128 : (i + 1) * 128])
    asked[...] = wanted.reshape(n_hst, 1, 128)
    request[n_hst - 1] = asked[me]

    pl.semaphore_wait(barrier, n_hst - 1 + n_dev - 1)

    def ask(k, carry):
        to = group_at(k, 1)
        pltpu.make_async_remote_copy(
            src_ref=asked.at[to],
            dst_ref=request.at[k],
            send_sem=ask_send,
            recv_sem=ask_recv,
            device_id={"hst": to, "dev": dev},
        ).start()
        return carry

    lax.fori_loop(0, n_hst - 1, ask, 0)

    def share(k, carry):
        pltpu.make_async_remote_copy(
            src_ref=cache.at[pl.ds(pl.multiple_of(core * half, half), half)],
            dst_ref=cached.at[core, k],
            send_sem=ag_send,
            recv_sem=ag_recv,
            device_id={"hst": me, "dev": lax.rem(dev + k, n_dev)},
        ).start()
        return carry

    lax.fori_loop(1, n_dev, share, 0)

    collected = hits + misses
    users = history_len.shape[0]
    hist = history_ids.shape[1]
    counts = []
    for u in range(users):
        ids = history_ids[u : u + 1, :].astype(F32)
        ids = jnp.where(iota((1, hist), 1) < history_len[u], ids, -1.0)
        col = jnp.concatenate([columns(ids[:, i * 128 : (i + 1) * 128]) for i in range(hist // 128)], axis=0)
        same = col == iota((hist, collected), 1).astype(F32)
        counts.append(jnp.sum(jnp.where(same, 1.0, 0.0), axis=0, keepdims=True))
    cand_col = columns(candidate_ids[...].astype(F32))
    of_hits = onehot(cand_col, hits)
    of_misses = onehot(cand_col - float(hits), misses)

    all_but_self = pl.ds(0, n_hst - 1)
    own_group = {"hst": me, "dev": dev}

    def whole(ref, sem_send, sem_recv):
        return pltpu.make_async_remote_copy(
            src_ref=ref, dst_ref=ref, send_sem=sem_send, recv_sem=sem_recv, device_id=own_group
        )

    whole(request.at[all_but_self], ask_send, ask_recv).wait_recv()

    def answer(i, carry):
        ids = request[pl.ds(i * chunk, chunk)]
        pick = iota((chunk, CAP, 128), 1) == iota((chunk, CAP, 128), 2)
        spread = jnp.where(pick, jnp.broadcast_to(ids, (chunk, CAP, 128)), 0.0)
        col = jnp.sum(spread, axis=-1, keepdims=True).reshape(chunk * CAP, 1)
        rows = dot(onehot(col, cold.shape[0]), cold[...]).astype(BF16)
        rows = rows.reshape(chunk, CAP, width)
        reply[pl.ds(i * chunk, chunk), 0:CAP, :] = rows[:, :, :half_w]
        reply[pl.ds(i * chunk, chunk), CAP:, :] = rows[:, :, half_w:]

        def send(k, inner):
            pltpu.make_async_remote_copy(
                src_ref=reply.at[k],
                dst_ref=arrived.at[k],
                send_sem=row_send,
                recv_sem=row_recv.at[i],
                device_id={"hst": group_at(k, -1), "dev": dev},
            ).start()
            return inner

        return lax.fori_loop(i * chunk, jnp.minimum((i + 1) * chunk, n_hst - 1), send, carry)

    lax.fori_loop(0, chunks, answer, 0)
    arrived[n_hst - 1] = reply[n_hst - 1]

    others = pl.ds(1, n_dev - 1)
    whole(cached.at[core, others], ag_send, ag_recv).wait_recv()
    swap = pltpu.make_async_remote_copy(
        src_ref=cached.at[core, others],
        dst_ref=cached.at[core, others],
        send_sem=swap_send,
        recv_sem=swap_recv,
        device_id={"hst": z * 2 + 1 - core, "dev": dev},
    )
    swap.start()
    cached[0, 0] = cache[0:half]
    cached[1, 0] = cache[half:]
    for w in weights:
        w.wait()
    heads_col = jnp.sum(w_out[...].astype(F32) * w_score[...], axis=-1, keepdims=True)
    eye = iota((128, 128), 0) == iota((128, 128), 1)
    head_row = jnp.concatenate(
        [
            jnp.sum(jnp.where(eye, heads_col[i * 128 : (i + 1) * 128], 0.0), axis=0, keepdims=True)
            for i in range(width // 128)
        ],
        axis=1,
    )
    peers, slots = hit_ids.shape
    ids = hit_ids[...]
    peer = iota((peers, slots), 0)
    place = (ids // half) * (peers * half) + lax.rem(dev - peer + peers, peers) * half + lax.rem(ids, half)
    spread = jnp.where(
        (iota((slots, slots), 0) == iota((slots, slots), 1))[None],
        jnp.broadcast_to(place.astype(F32)[:, None, :], (peers, slots, slots)),
        0.0,
    )
    place_col = jnp.sum(spread, axis=-1, keepdims=True).reshape(hits, 1)
    whole(cached.at[1 - core, others], swap_send, swap_recv).wait_recv()
    x_hit = dot(onehot(place_col, 2 * peers * half), cached[...].reshape(2 * peers * half, width)).astype(BF16)
    normed = normalize(x_hit.astype(F32)).astype(BF16)
    kv[0:hits] = silu_of_double(0.5 * dot(normed, w_kv[...])).astype(BF16)
    cand_x = dot(of_hits, x_hit)

    o = owner_col.astype(jnp.int32)
    chip = lax.rem(o // 2 - z + nz, nz)
    pair = jnp.where(chip >= far, 2 * (chip - far), 2 * (far - chip) - 1)
    order = 2 * pair + 1 - lax.rem(o + core, 2)
    seat_col = (order * CAP).astype(F32) + slot_col
    left = jnp.zeros((misses, half_w), F32)
    right = jnp.zeros((misses, half_w), F32)
    for i in range(chunks):
        n = chunk - (i == chunks - 1)
        whole(arrived.at[pl.ds(i * chunk, n)], row_send, row_recv.at[i]).wait_recv()
        pick = onehot(seat_col - float(i * chunk * CAP), chunk * CAP)
        part = arrived[pl.ds(i * chunk, chunk)]
        left = left + dot(pick, part[:, 0:CAP, :].reshape(chunk * CAP, half_w))
        right = right + dot(pick, part[:, CAP:, :].reshape(chunk * CAP, half_w))
    x_miss32 = jnp.concatenate([left, right], axis=1)
    x_miss = x_miss32.astype(BF16)
    cand_x = cand_x + dot(of_misses, x_miss)
    normed = normalize(x_miss32).astype(BF16)
    kv[hits:] = silu_of_double(0.5 * dot(normed, w_kv[...])).astype(BF16)

    cand_n = normalize(cand_x).astype(BF16)
    proj = silu_of_double(0.5 * dot(cand_n, w_cand[...])).astype(BF16)
    cands = candidate_ids.shape[1]
    scale = 1.0 / math.sqrt(DH)
    attended = []
    for h in range(HEADS):
        cols = slice(h * DH, (h + 1) * DH)
        at = lambda b: proj[:, b * width + h * DH : b * width + (h + 1) * DH]
        query = at(2)
        half_raw = dot_nt(query, kv[:, cols]) * (0.5 * scale)
        act = silu_of_double(half_raw)
        weight = jnp.concatenate(
            [(act[u * cands : (u + 1) * cands] * counts[u]).astype(BF16) for u in range(users)], axis=0
        )
        summed = dot(weight, kv[:, width + h * DH : width + (h + 1) * DH])
        own = jnp.sum(query.astype(F32) * at(3).astype(F32), axis=-1, keepdims=True) * (0.5 * scale)
        mine = silu_of_double(own) * at(1).astype(F32)
        shares = [
            summed[u * cands : (u + 1) * cands] / history_len[u].astype(F32) for u in range(users)
        ]
        attended.append(jnp.concatenate(shares, axis=0) + mine)
    mixed = normalize(jnp.concatenate(attended, axis=1)) * proj[:, :width].astype(F32)
    score = jnp.sum(cand_x * w_score[...] + mixed * head_row, axis=-1, keepdims=True)
    eye = iota((cands, cands), 0) == iota((cands, cands), 1)
    for u in range(users):
        out[u : u + 1, :] = jnp.sum(
            jnp.where(eye, score[u * cands : (u + 1) * cands], 0.0), axis=0, keepdims=True
        )

    whole(asked.at[all_but_self], ask_send, ask_recv).wait_send()
    whole(reply.at[all_but_self], row_send, row_recv.at[0]).wait_send()
    whole(cached.at[core, others], ag_send, ag_recv).wait_send()
    swap.wait_send()


def per_device(
    n_hst,
    n_dev,
    cache_table,
    cold_table,
    hit_ids,
    miss_owner,
    miss_row,
    history_ids,
    candidate_ids,
    history_len,
    w_kv,
    w_cand,
    w_out,
    w_score,
):
    width = cache_table.shape[1]
    misses = miss_row.shape[0]
    collected = hit_ids.size + misses
    half = cache_table.shape[0] // 2
    chunks = 4
    vmem = pl.BlockSpec(memory_space=pltpu.VMEM)
    smem = pl.BlockSpec(memory_space=pltpu.SMEM)
    hbm = pl.BlockSpec(memory_space=pl.ANY)
    dma = pltpu.SemaphoreType.DMA
    return pl.pallas_call(
        functools.partial(kernel, n_hst, n_dev),
        out_shape=jax.ShapeDtypeStruct(candidate_ids.shape, F32),
        in_specs=[vmem] * 7 + [smem] + [hbm] * 3 + [vmem],
        out_specs=vmem,
        scratch_shapes=[
            pltpu.VMEM(w_kv.shape, BF16),
            pltpu.VMEM(w_cand.shape, BF16),
            pltpu.VMEM(w_out.shape, BF16),
            pltpu.VMEM((n_hst, 1, 128), F32),
            pltpu.VMEM((n_hst, 1, 128), F32),
            pltpu.VMEM((n_hst, 2 * CAP, width // 2), BF16),
            pltpu.VMEM((n_hst, 2 * CAP, width // 2), BF16),
            pltpu.VMEM((2, n_dev, half, width), BF16),
            pltpu.VMEM((collected, 2 * width), BF16),
            dma((3,)),
            dma,
            dma,
            dma,
            dma((chunks,)),
            dma,
            dma,
            dma,
            dma,
        ],
        compiler_params=pltpu.CompilerParams(
            collective_id=0, has_side_effects=True, vmem_limit_bytes=48 * 1024 * 1024
        ),
    )(
        cache_table,
        cold_table,
        hit_ids,
        miss_owner.reshape(misses // 128, 128),
        miss_row.reshape(misses // 128, 128),
        history_ids,
        candidate_ids,
        history_len,
        w_kv,
        w_cand,
        w_out,
        w_score.reshape(1, width),
    )


def solution(mesh):
    rows = P(("hst", "dev"), None)
    placed = (
        P("dev", None),
        rows,
        rows,
        rows,
        P(("hst", "dev")),
        rows,
        rows,
        P(("hst", "dev")),
        P(),
        P(),
        P(),
        P(),
    )
    return jax.shard_map(
        functools.partial(per_device, mesh.shape["hst"], mesh.shape["dev"]),
        mesh=mesh,
        in_specs=placed,
        out_specs=rows,
        check_vma=False,
    )
```

```python
import functools
import math

import jax
import jax.numpy as jnp
from jax import lax
from jax.experimental import pallas as pl
from jax.experimental.pallas import tpu as pltpu
from jax.sharding import PartitionSpec as P

F32 = jnp.float32
BF16 = jnp.bfloat16
HEADS = 4
DH = 128
CAP = 8
EPS = 1e-05
STARTS = (3, 7, 11, 14)


def iota(shape, dim):
    return lax.broadcasted_iota(jnp.int32, shape, dim)


def normalize(x):
    centered = x - jnp.mean(x, axis=-1, keepdims=True)
    var = jnp.mean(centered * centered, axis=-1, keepdims=True)
    return centered * lax.rsqrt(var + EPS)


def silu_of_double(y):
    return y + y * jnp.tanh(y)


def dot(a, b):
    return jnp.dot(a, b, preferred_element_type=F32)


def dot_nt(a, b):
    return lax.dot_general(a, b, (((1,), (1,)), ((), ())), preferred_element_type=F32)


def columns(rows):
    r, n = rows.shape
    eye = iota((n, n), 0) == iota((n, n), 1)
    spread = jnp.where(eye[None], jnp.broadcast_to(rows[:, None, :], (r, n, n)), 0.0)
    return jnp.sum(spread, axis=-1, keepdims=True).reshape(r * n, 1)


def onehot(column, width):
    lanes = iota((column.shape[0], width), 1).astype(F32)
    return jnp.where(column == lanes, 1.0, 0.0).astype(BF16)


def kernel(
    n_hst,
    n_dev,
    *refs,
):
    inputs, out, held, scratch = refs[:12], refs[12], refs[13:25], refs[25:]
    (cache, cold, hit_ids, owner, miss_row, history_ids, candidate_ids, history_len) = held[:8]
    w_kv, w_cand, w_out, w_score = held[8:]
    (
        asked,
        request,
        reply,
        arrived,
        cached,
        kv,
        load_sem,
        ask_send,
        ask_recv,
        row_send,
        row_recv,
        ag_send,
        ag_recv,
        swap_send,
        swap_recv,
    ) = scratch
    me = lax.axis_index("hst")
    dev = lax.axis_index("dev")
    z, core = me // 2, lax.rem(me, 2)
    nz = n_hst // 2
    far = nz // 2
    hits = hit_ids.shape[0] * hit_ids.shape[1]
    misses = owner.shape[0] * owner.shape[1]
    width = cache.shape[1]
    half_w = width // 2
    users = history_len.shape[0]
    half = cache.shape[0] // 2
    seats = lambda top: 2 + 4 * (far - top - 1) if top < far else 0
    tops = [far] + [max(1, far - n) for n in STARTS]
    chunks = []
    for high, low in zip(tops, tops[1:] + [0]):
        chunks.append((high, low, seats(high), seats(low) if low else n_hst))

    def each_group(high, low, act):
        if high == far:
            chip = lax.rem(z + far, nz)
            act(0, chip, chip, 1 - core)
            act(1, chip, chip, core)
            high = far - 1

        def step(i, carry):
            d = high - i
            up, down = lax.rem(z + d, nz), lax.rem(z + nz - d, nz)
            seat = 2 + 4 * (far - 1 - d)
            act(seat, up, down, 1 - core)
            act(seat + 1, up, down, core)
            act(seat + 2, down, up, 1 - core)
            act(seat + 3, down, up, core)
            return carry

        lax.fori_loop(0, high - max(low, 0), step, 0)
        if low == 0:
            act(n_hst - 2, z, z, 1 - core)

    loads = [
        pltpu.make_async_copy(source, target, load_sem.at[i])
        for i, (source, target) in enumerate(zip(inputs, held))
    ]
    loads[3].start()
    loads[4].start()
    barrier = pltpu.get_barrier_semaphore()

    def greet(seat, chip, back, side):
        pl.semaphore_signal(barrier, inc=1, device_id={"hst": chip * 2 + side, "dev": dev})

    each_group(far, 0, greet)

    def greet_dev(k, carry):
        pl.semaphore_signal(barrier, inc=1, device_id={"hst": me, "dev": lax.rem(dev + k, n_dev)})
        return carry

    lax.fori_loop(1, n_dev, greet_dev, 0)
    for i in (1, 0, 2, 5, 6, 7, 11, 8, 9, 10):
        loads[i].start()

    loads[3].wait()
    loads[4].wait()
    owners = owner[...].astype(F32)
    owner_col = columns(owners)
    row_col = columns(miss_row[...].astype(F32))
    by_miss = onehot(owner_col, 128)
    earlier = jnp.where(iota((misses, misses), 1) < iota((misses, misses), 0), 1.0, 0.0).astype(BF16)
    before = dot(earlier, by_miss)
    slot_col = jnp.sum(before * by_miss.astype(F32), axis=-1, keepdims=True)
    lanes = iota((misses, 128), 1).astype(F32)
    rows_at_slot = jnp.where(slot_col == lanes, row_col, 0.0).astype(BF16)
    wanted = jnp.zeros((n_hst, 128), F32)
    groups = iota((n_hst, 128), 0).astype(F32)
    for i in range(misses // 128):
        by_group = jnp.where(owners[i : i + 1] == groups, 1.0, 0.0).astype(BF16)
        wanted = wanted + dot(by_group, rows_at_slot[i * 128 : (i + 1) * 128])
    asked[...] = wanted.reshape(n_hst, 1, 128)
    request[n_hst - 1] = asked[me]

    pl.semaphore_wait(barrier, n_hst - 1 + n_dev - 1)

    for j, (high, low, _, _) in enumerate(chunks):

        def ask(seat, chip, back, side):
            pltpu.make_async_remote_copy(
                src_ref=asked.at[chip * 2 + side],
                dst_ref=request.at[seat],
                send_sem=ask_send,
                recv_sem=ask_recv.at[j],
                device_id={"hst": chip * 2 + side, "dev": dev},
            ).start()

        each_group(high, low, ask)
    loads[0].wait()

    def share(k, carry):
        pltpu.make_async_remote_copy(
            src_ref=cache.at[pl.ds(pl.multiple_of(core * half, half), half)],
            dst_ref=cached.at[core, k],
            send_sem=ag_send,
            recv_sem=ag_recv,
            device_id={"hst": me, "dev": lax.rem(dev + k, n_dev)},
        ).start()
        return carry

    lax.fori_loop(1, n_dev, share, 0)

    all_but_self = pl.ds(0, n_hst - 1)
    own_group = {"hst": me, "dev": dev}

    def whole(ref, sem_send, sem_recv):
        return pltpu.make_async_remote_copy(
            src_ref=ref, dst_ref=ref, send_sem=sem_send, recv_sem=sem_recv, device_id=own_group
        )

    others = pl.ds(1, n_dev - 1)
    peers, slots = hit_ids.shape

    def count_rows():
        for i in (2, 5, 6, 7):
            loads[i].wait()
        collected = hits + misses
        hist = history_ids.shape[1]
        counts = []
        for u in range(users):
            ids = history_ids[u : u + 1, :].astype(F32)
            ids = jnp.where(iota((1, hist), 1) < history_len[u], ids, -1.0)
            col = jnp.concatenate([columns(ids[:, i * 128 : (i + 1) * 128]) for i in range(hist // 128)], axis=0)
            same = col == iota((hist, collected), 1).astype(F32)
            counts.append(jnp.sum(jnp.where(same, 1.0, 0.0), axis=0, keepdims=True))
        cand_col = columns(candidate_ids[...].astype(F32))
        of_hits = onehot(cand_col, hits)
        of_misses = onehot(cand_col - float(hits), misses)
        return counts, of_hits, of_misses

    def pass_cache():
        whole(cached.at[core, others], ag_send, ag_recv).wait_recv()
        swap = pltpu.make_async_remote_copy(
            src_ref=cached.at[core, others],
            dst_ref=cached.at[core, others],
            send_sem=swap_send,
            recv_sem=swap_recv,
            device_id={"hst": z * 2 + 1 - core, "dev": dev},
        )
        swap.start()
        cached[0, 0] = cache[0:half]
        cached[1, 0] = cache[half:]
        return swap

    def place_hits():
        for i in (8, 9, 10, 11):
            loads[i].wait()
        heads_col = jnp.sum(w_out[...].astype(F32) * w_score[...], axis=-1, keepdims=True)
        eye = iota((128, 128), 0) == iota((128, 128), 1)
        head_row = jnp.concatenate(
            [
                jnp.sum(jnp.where(eye, heads_col[i * 128 : (i + 1) * 128], 0.0), axis=0, keepdims=True)
                for i in range(width // 128)
            ],
            axis=1,
        )
        ids = hit_ids[...]
        peer = iota((peers, slots), 0)
        place = (ids // half) * (peers * half) + lax.rem(dev - peer + peers, peers) * half + lax.rem(ids, half)
        spread = jnp.where(
            (iota((slots, slots), 0) == iota((slots, slots), 1))[None],
            jnp.broadcast_to(place.astype(F32)[:, None, :], (peers, slots, slots)),
            0.0,
        )
        place_col = jnp.sum(spread, axis=-1, keepdims=True).reshape(hits, 1)
        return head_row, place_col

    def take_hits(of_hits, place_col):
        whole(cached.at[1 - core, others], swap_send, swap_recv).wait_recv()
        x_hit = dot(onehot(place_col, 2 * peers * half), cached[...].reshape(2 * peers * half, width)).astype(BF16)
        normed = normalize(x_hit.astype(F32)).astype(BF16)
        kv[0:hits] = silu_of_double(0.5 * dot(normed, w_kv[...])).astype(BF16)
        cand_x = dot(of_hits, x_hit)
        return cand_x

    loads[1].wait()
    for j, (high, low, first, end) in enumerate(chunks):
        n = end - first
        whole(request.at[pl.ds(first, min(end, n_hst - 1) - first)], ask_send, ask_recv.at[j]).wait_recv()
        ids = request[first:end]
        pick = iota((n, CAP, 128), 1) == iota((n, CAP, 128), 2)
        spread = jnp.where(pick, jnp.broadcast_to(ids, (n, CAP, 128)), 0.0)
        col = jnp.sum(spread, axis=-1, keepdims=True).reshape(n * CAP, 1)
        rows = dot(onehot(col, cold.shape[0]), cold[...]).astype(BF16).reshape(n, CAP, width)
        reply[first:end, 0:CAP, :] = rows[:, :, :half_w]
        reply[first:end, CAP:, :] = rows[:, :, half_w:]

        def answer(seat, chip, back, side):
            pltpu.make_async_remote_copy(
                src_ref=reply.at[seat],
                dst_ref=arrived.at[seat],
                send_sem=row_send,
                recv_sem=row_recv.at[j],
                device_id={"hst": back * 2 + side, "dev": dev},
            ).start()

        each_group(high, low, answer)
        if j == 0:
            counts, of_hits, of_misses = count_rows()
            swap = pass_cache()
        if j == 1:
            head_row, place_col = place_hits()
        if j == 2:
            cand_x = take_hits(of_hits, place_col)
    arrived[n_hst - 1] = reply[n_hst - 1]

    o = owner_col.astype(jnp.int32)
    chip = lax.rem(o // 2 - z + nz, nz)
    pair = jnp.where(chip >= far, 2 * (chip - far), 2 * (far - chip) - 1)
    order = 2 * pair + 1 - lax.rem(o + core, 2)
    seat_col = (order * CAP).astype(F32) + slot_col
    left = jnp.zeros((misses, half_w), F32)
    right = jnp.zeros((misses, half_w), F32)
    for j, (_, _, first, end) in enumerate(chunks):
        n = end - first
        whole(arrived.at[pl.ds(first, min(end, n_hst - 1) - first)], row_send, row_recv.at[j]).wait_recv()
        pick = onehot(seat_col - float(first * CAP), n * CAP)
        part = arrived[first:end]
        left = left + dot(pick, part[:, 0:CAP, :].reshape(n * CAP, half_w))
        right = right + dot(pick, part[:, CAP:, :].reshape(n * CAP, half_w))
    x_miss32 = jnp.concatenate([left, right], axis=1)
    x_miss = x_miss32.astype(BF16)
    cand_x = cand_x + dot(of_misses, x_miss)
    normed = normalize(x_miss32).astype(BF16)
    kv[hits:] = silu_of_double(0.5 * dot(normed, w_kv[...])).astype(BF16)

    cand_n = normalize(cand_x).astype(BF16)
    proj = silu_of_double(0.5 * dot(cand_n, w_cand[...])).astype(BF16)
    cands = candidate_ids.shape[1]
    scale = 1.0 / math.sqrt(DH)
    attended = []
    for h in range(HEADS):
        cols = slice(h * DH, (h + 1) * DH)
        at = lambda b: proj[:, b * width + h * DH : b * width + (h + 1) * DH]
        query = at(2)
        half_raw = dot_nt(query, kv[:, cols]) * (0.5 * scale)
        act = silu_of_double(half_raw)
        weight = jnp.concatenate(
            [(act[u * cands : (u + 1) * cands] * counts[u]).astype(BF16) for u in range(users)], axis=0
        )
        summed = dot(weight, kv[:, width + h * DH : width + (h + 1) * DH])
        own = jnp.sum(query.astype(F32) * at(3).astype(F32), axis=-1, keepdims=True) * (0.5 * scale)
        mine = silu_of_double(own) * at(1).astype(F32)
        shares = [
            summed[u * cands : (u + 1) * cands] / history_len[u].astype(F32) for u in range(users)
        ]
        attended.append(jnp.concatenate(shares, axis=0) + mine)
    mixed = normalize(jnp.concatenate(attended, axis=1)) * proj[:, :width].astype(F32)
    score = jnp.sum(cand_x * w_score[...] + mixed * head_row, axis=-1, keepdims=True)
    eye = iota((cands, cands), 0) == iota((cands, cands), 1)
    for u in range(users):
        out[u : u + 1, :] = jnp.sum(
            jnp.where(eye, score[u * cands : (u + 1) * cands], 0.0), axis=0, keepdims=True
        )

    whole(asked.at[all_but_self], ask_send, ask_recv.at[0]).wait_send()
    whole(reply.at[all_but_self], row_send, row_recv.at[0]).wait_send()
    whole(cached.at[core, others], ag_send, ag_recv).wait_send()
    swap.wait_send()


def per_device(
    n_hst,
    n_dev,
    cache_table,
    cold_table,
    hit_ids,
    miss_owner,
    miss_row,
    history_ids,
    candidate_ids,
    history_len,
    w_kv,
    w_cand,
    w_out,
    w_score,
):
    width = cache_table.shape[1]
    misses = miss_row.shape[0]
    collected = hit_ids.size + misses
    half = cache_table.shape[0] // 2
    chunks = 1 + len(STARTS)
    operands = (
        cache_table,
        cold_table,
        hit_ids,
        miss_owner.reshape(misses // 128, 128),
        miss_row.reshape(misses // 128, 128),
        history_ids,
        candidate_ids,
        history_len,
        w_kv,
        w_cand,
        w_out,
        w_score.reshape(1, width),
    )
    spaces = [pltpu.VMEM] * 7 + [pltpu.SMEM] + [pltpu.VMEM] * 4
    dma = pltpu.SemaphoreType.DMA
    return pl.pallas_call(
        functools.partial(kernel, n_hst, n_dev),
        out_shape=jax.ShapeDtypeStruct(candidate_ids.shape, F32),
        in_specs=[pl.BlockSpec(memory_space=pltpu.HBM)] * len(operands),
        out_specs=pl.BlockSpec(memory_space=pltpu.VMEM),
        scratch_shapes=[
            *[space(a.shape, a.dtype) for space, a in zip(spaces, operands)],
            pltpu.VMEM((n_hst, 1, 128), F32),
            pltpu.VMEM((n_hst, 1, 128), F32),
            pltpu.VMEM((n_hst, 2 * CAP, width // 2), BF16),
            pltpu.VMEM((n_hst, 2 * CAP, width // 2), BF16),
            pltpu.VMEM((2, n_dev, half, width), BF16),
            pltpu.VMEM((collected, 2 * width), BF16),
            dma((len(operands),)),
            dma,
            dma((chunks,)),
            dma,
            dma((chunks,)),
            dma,
            dma,
            dma,
            dma,
        ],
        compiler_params=pltpu.CompilerParams(
            collective_id=0, has_side_effects=True, vmem_limit_bytes=48 * 1024 * 1024
        ),
    )(*[pltpu.with_memory_space_constraint(a, pltpu.HBM) for a in operands])


def solution(mesh):
    rows = P(("hst", "dev"), None)
    placed = (
        P("dev", None),
        rows,
        rows,
        rows,
        P(("hst", "dev")),
        rows,
        rows,
        P(("hst", "dev")),
        P(),
        P(),
        P(),
        P(),
    )
    return jax.shard_map(
        functools.partial(per_device, mesh.shape["hst"], mesh.shape["dev"]),
        mesh=mesh,
        in_specs=placed,
        out_specs=rows,
        check_vma=False,
    )
```

```python
import functools
import math

import jax
import jax.numpy as jnp
from jax import lax
from jax.experimental import pallas as pl
from jax.experimental.pallas import tpu as pltpu
from jax.sharding import PartitionSpec as P

F32 = jnp.float32
BF16 = jnp.bfloat16
HEADS = 4
DH = 128
CAP = 8
EPS = 1e-05
STARTS = (3, 7, 11, 14)
ORDER = (4, 3, 0, 1, 2)


def iota(shape, dim):
    return lax.broadcasted_iota(jnp.int32, shape, dim)


def normalize(x):
    centered = x - jnp.mean(x, axis=-1, keepdims=True)
    var = jnp.mean(centered * centered, axis=-1, keepdims=True)
    return centered * lax.rsqrt(var + EPS)


def silu_of_double(y):
    return y + y * jnp.tanh(y)


def dot(a, b):
    return jnp.dot(a, b, preferred_element_type=F32)


def dot_nt(a, b):
    return lax.dot_general(a, b, (((1,), (1,)), ((), ())), preferred_element_type=F32)


def columns(rows):
    r, n = rows.shape
    eye = iota((n, n), 0) == iota((n, n), 1)
    spread = jnp.where(eye[None], jnp.broadcast_to(rows[:, None, :], (r, n, n)), 0.0)
    return jnp.sum(spread, axis=-1, keepdims=True).reshape(r * n, 1)


def onehot(column, width):
    lanes = iota((column.shape[0], width), 1).astype(F32)
    return jnp.where(column == lanes, 1.0, 0.0).astype(BF16)


def kernel(
    n_hst,
    n_dev,
    *refs,
):
    inputs, out, held, scratch = refs[:12], refs[12], refs[13:25], refs[25:]
    (cache, cold, hit_ids, owner, miss_row, history_ids, candidate_ids, history_len) = held[:8]
    w_kv, w_cand, w_out, w_score = held[8:]
    (
        asked,
        request,
        reply,
        arrived,
        cached,
        kv,
        load_sem,
        ask_send,
        ask_recv,
        row_send,
        row_recv,
        ag_send,
        ag_recv,
        swap_send,
        swap_recv,
    ) = scratch
    me = lax.axis_index("hst")
    dev = lax.axis_index("dev")
    z, core = me // 2, lax.rem(me, 2)
    nz = n_hst // 2
    far = nz // 2
    hits = hit_ids.shape[0] * hit_ids.shape[1]
    misses = owner.shape[0] * owner.shape[1]
    width = cache.shape[1]
    half_w = width // 2
    users = history_len.shape[0]
    half = cache.shape[0] // 2
    seats = lambda top: 2 + 4 * (far - top - 1) if top < far else 0
    tops = [far] + [max(1, far - n) for n in STARTS]
    chunks = []
    for high, low in zip(tops, tops[1:] + [0]):
        chunks.append((high, low, seats(high), seats(low) if low else n_hst))

    def each_group(high, low, act):
        if high == far:
            chip = lax.rem(z + far, nz)
            act(0, chip, chip, 1 - core)
            act(1, chip, chip, core)
            high = far - 1

        def step(i, carry):
            d = high - i
            up, down = lax.rem(z + d, nz), lax.rem(z + nz - d, nz)
            seat = 2 + 4 * (far - 1 - d)
            act(seat, up, down, 1 - core)
            act(seat + 1, up, down, core)
            act(seat + 2, down, up, 1 - core)
            act(seat + 3, down, up, core)
            return carry

        lax.fori_loop(0, high - max(low, 0), step, 0)
        if low == 0:
            act(n_hst - 2, z, z, 1 - core)

    loads = [
        pltpu.make_async_copy(source, target, load_sem.at[i])
        for i, (source, target) in enumerate(zip(inputs, held))
    ]
    loads[3].start()
    loads[4].start()
    barrier = pltpu.get_barrier_semaphore()

    def greet(seat, chip, back, side):
        pl.semaphore_signal(barrier, inc=1, device_id={"hst": chip * 2 + side, "dev": dev})

    each_group(far, 0, greet)

    def greet_dev(k, carry):
        pl.semaphore_signal(barrier, inc=1, device_id={"hst": me, "dev": lax.rem(dev + k, n_dev)})
        return carry

    lax.fori_loop(1, n_dev, greet_dev, 0)
    for i in (1, 0, 2, 5, 6, 7, 11, 8, 9, 10):
        loads[i].start()

    loads[3].wait()
    loads[4].wait()
    owners = owner[...].astype(F32)
    owner_col = columns(owners)
    row_col = columns(miss_row[...].astype(F32))
    by_miss = onehot(owner_col, 128)
    earlier = jnp.where(iota((misses, misses), 1) < iota((misses, misses), 0), 1.0, 0.0).astype(BF16)
    before = dot(earlier, by_miss)
    slot_col = jnp.sum(before * by_miss.astype(F32), axis=-1, keepdims=True)
    lanes = iota((misses, 128), 1).astype(F32)
    rows_at_slot = jnp.where(slot_col == lanes, row_col, 0.0).astype(BF16)
    wanted = jnp.zeros((n_hst, 128), F32)
    groups = iota((n_hst, 128), 0).astype(F32)
    for i in range(misses // 128):
        by_group = jnp.where(owners[i : i + 1] == groups, 1.0, 0.0).astype(BF16)
        wanted = wanted + dot(by_group, rows_at_slot[i * 128 : (i + 1) * 128])
    asked[...] = wanted.reshape(n_hst, 1, 128)
    request[n_hst - 1] = asked[me]

    pl.semaphore_wait(barrier, n_hst - 1 + n_dev - 1)

    for j, (high, low, _, _) in enumerate(chunks):

        def ask(seat, chip, back, side):
            pltpu.make_async_remote_copy(
                src_ref=asked.at[chip * 2 + side],
                dst_ref=request.at[seat],
                send_sem=ask_send,
                recv_sem=ask_recv.at[j],
                device_id={"hst": chip * 2 + side, "dev": dev},
            ).start()

        each_group(high, low, ask)
    loads[0].wait()

    def share(k, carry):
        pltpu.make_async_remote_copy(
            src_ref=cache.at[pl.ds(pl.multiple_of(core * half, half), half)],
            dst_ref=cached.at[core, k],
            send_sem=ag_send,
            recv_sem=ag_recv,
            device_id={"hst": me, "dev": lax.rem(dev + k, n_dev)},
        ).start()
        return carry

    lax.fori_loop(1, n_dev, share, 0)

    all_but_self = pl.ds(0, n_hst - 1)
    own_group = {"hst": me, "dev": dev}

    def whole(ref, sem_send, sem_recv):
        return pltpu.make_async_remote_copy(
            src_ref=ref, dst_ref=ref, send_sem=sem_send, recv_sem=sem_recv, device_id=own_group
        )

    others = pl.ds(1, n_dev - 1)
    peers, slots = hit_ids.shape

    def count_rows():
        for i in (2, 5, 6, 7):
            loads[i].wait()
        collected = hits + misses
        hist = history_ids.shape[1]
        counts = []
        for u in range(users):
            ids = history_ids[u : u + 1, :].astype(F32)
            ids = jnp.where(iota((1, hist), 1) < history_len[u], ids, -1.0)
            col = jnp.concatenate([columns(ids[:, i * 128 : (i + 1) * 128]) for i in range(hist // 128)], axis=0)
            same = col == iota((hist, collected), 1).astype(F32)
            counts.append(jnp.sum(jnp.where(same, 1.0, 0.0), axis=0, keepdims=True))
        cand_col = columns(candidate_ids[...].astype(F32))
        of_hits = onehot(cand_col, hits)
        of_misses = onehot(cand_col - float(hits), misses)
        return counts, of_hits, of_misses

    def pass_cache():
        whole(cached.at[core, others], ag_send, ag_recv).wait_recv()
        swap = pltpu.make_async_remote_copy(
            src_ref=cached.at[core, others],
            dst_ref=cached.at[core, others],
            send_sem=swap_send,
            recv_sem=swap_recv,
            device_id={"hst": z * 2 + 1 - core, "dev": dev},
        )
        swap.start()
        cached[0, 0] = cache[0:half]
        cached[1, 0] = cache[half:]
        return swap

    def place_hits():
        for i in (8, 9, 10, 11):
            loads[i].wait()
        heads_col = jnp.sum(w_out[...].astype(F32) * w_score[...], axis=-1, keepdims=True)
        eye = iota((128, 128), 0) == iota((128, 128), 1)
        head_row = jnp.concatenate(
            [
                jnp.sum(jnp.where(eye, heads_col[i * 128 : (i + 1) * 128], 0.0), axis=0, keepdims=True)
                for i in range(width // 128)
            ],
            axis=1,
        )
        ids = hit_ids[...]
        peer = iota((peers, slots), 0)
        place = (ids // half) * (peers * half) + lax.rem(dev - peer + peers, peers) * half + lax.rem(ids, half)
        spread = jnp.where(
            (iota((slots, slots), 0) == iota((slots, slots), 1))[None],
            jnp.broadcast_to(place.astype(F32)[:, None, :], (peers, slots, slots)),
            0.0,
        )
        place_col = jnp.sum(spread, axis=-1, keepdims=True).reshape(hits, 1)
        return head_row, place_col

    def take_hits(of_hits, place_col):
        whole(cached.at[1 - core, others], swap_send, swap_recv).wait_recv()
        x_hit = dot(onehot(place_col, 2 * peers * half), cached[...].reshape(2 * peers * half, width)).astype(BF16)
        normed = normalize(x_hit.astype(F32)).astype(BF16)
        kv[0:hits] = silu_of_double(0.5 * dot(normed, w_kv[...])).astype(BF16)
        cand_x = dot(of_hits, x_hit)
        return cand_x

    loads[1].wait()
    for turn, j in enumerate(ORDER):
        high, low, first, end = chunks[j]
        n = end - first
        whole(request.at[pl.ds(first, min(end, n_hst - 1) - first)], ask_send, ask_recv.at[j]).wait_recv()
        ids = request[first:end]
        pick = iota((n, CAP, 128), 1) == iota((n, CAP, 128), 2)
        spread = jnp.where(pick, jnp.broadcast_to(ids, (n, CAP, 128)), 0.0)
        col = jnp.sum(spread, axis=-1, keepdims=True).reshape(n * CAP, 1)
        rows = dot(onehot(col, cold.shape[0]), cold[...]).astype(BF16).reshape(n, CAP, width)
        reply[first:end, 0:CAP, :] = rows[:, :, :half_w]
        reply[first:end, CAP:, :] = rows[:, :, half_w:]

        def answer(seat, chip, back, side):
            pltpu.make_async_remote_copy(
                src_ref=reply.at[seat],
                dst_ref=arrived.at[seat],
                send_sem=row_send,
                recv_sem=row_recv.at[j],
                device_id={"hst": back * 2 + side, "dev": dev},
            ).start()

        each_group(high, low, answer)
        if turn == 2:
            counts, of_hits, of_misses = count_rows()
            swap = pass_cache()
        if turn == 3:
            head_row, place_col = place_hits()
        if turn == 4:
            cand_x = take_hits(of_hits, place_col)
    arrived[n_hst - 1] = reply[n_hst - 1]

    o = owner_col.astype(jnp.int32)
    chip = lax.rem(o // 2 - z + nz, nz)
    pair = jnp.where(chip >= far, 2 * (chip - far), 2 * (far - chip) - 1)
    order = 2 * pair + 1 - lax.rem(o + core, 2)
    seat_col = (order * CAP).astype(F32) + slot_col
    left = jnp.zeros((misses, half_w), F32)
    right = jnp.zeros((misses, half_w), F32)
    for j in ORDER:
        _, _, first, end = chunks[j]
        n = end - first
        whole(arrived.at[pl.ds(first, min(end, n_hst - 1) - first)], row_send, row_recv.at[j]).wait_recv()
        pick = onehot(seat_col - float(first * CAP), n * CAP)
        part = arrived[first:end]
        left = left + dot(pick, part[:, 0:CAP, :].reshape(n * CAP, half_w))
        right = right + dot(pick, part[:, CAP:, :].reshape(n * CAP, half_w))
    x_miss32 = jnp.concatenate([left, right], axis=1)
    x_miss = x_miss32.astype(BF16)
    cand_x = cand_x + dot(of_misses, x_miss)
    normed = normalize(x_miss32).astype(BF16)
    kv[hits:] = silu_of_double(0.5 * dot(normed, w_kv[...])).astype(BF16)

    cand_n = normalize(cand_x).astype(BF16)
    proj = silu_of_double(0.5 * dot(cand_n, w_cand[...])).astype(BF16)
    cands = candidate_ids.shape[1]
    scale = 1.0 / math.sqrt(DH)
    attended = []
    for h in range(HEADS):
        cols = slice(h * DH, (h + 1) * DH)
        at = lambda b: proj[:, b * width + h * DH : b * width + (h + 1) * DH]
        query = at(2)
        half_raw = dot_nt(query, kv[:, cols]) * (0.5 * scale)
        act = silu_of_double(half_raw)
        weight = jnp.concatenate(
            [(act[u * cands : (u + 1) * cands] * counts[u]).astype(BF16) for u in range(users)], axis=0
        )
        summed = dot(weight, kv[:, width + h * DH : width + (h + 1) * DH])
        own = jnp.sum(query.astype(F32) * at(3).astype(F32), axis=-1, keepdims=True) * (0.5 * scale)
        mine = silu_of_double(own) * at(1).astype(F32)
        shares = [
            summed[u * cands : (u + 1) * cands] / history_len[u].astype(F32) for u in range(users)
        ]
        attended.append(jnp.concatenate(shares, axis=0) + mine)
    mixed = normalize(jnp.concatenate(attended, axis=1)) * proj[:, :width].astype(F32)
    score = jnp.sum(cand_x * w_score[...] + mixed * head_row, axis=-1, keepdims=True)
    eye = iota((cands, cands), 0) == iota((cands, cands), 1)
    for u in range(users):
        out[u : u + 1, :] = jnp.sum(
            jnp.where(eye, score[u * cands : (u + 1) * cands], 0.0), axis=0, keepdims=True
        )

    whole(asked.at[all_but_self], ask_send, ask_recv.at[0]).wait_send()
    whole(reply.at[all_but_self], row_send, row_recv.at[0]).wait_send()
    whole(cached.at[core, others], ag_send, ag_recv).wait_send()
    swap.wait_send()


def per_device(
    n_hst,
    n_dev,
    cache_table,
    cold_table,
    hit_ids,
    miss_owner,
    miss_row,
    history_ids,
    candidate_ids,
    history_len,
    w_kv,
    w_cand,
    w_out,
    w_score,
):
    width = cache_table.shape[1]
    misses = miss_row.shape[0]
    collected = hit_ids.size + misses
    half = cache_table.shape[0] // 2
    chunks = 1 + len(STARTS)
    operands = (
        cache_table,
        cold_table,
        hit_ids,
        miss_owner.reshape(misses // 128, 128),
        miss_row.reshape(misses // 128, 128),
        history_ids,
        candidate_ids,
        history_len,
        w_kv,
        w_cand,
        w_out,
        w_score.reshape(1, width),
    )
    spaces = [pltpu.VMEM] * 7 + [pltpu.SMEM] + [pltpu.VMEM] * 4
    dma = pltpu.SemaphoreType.DMA
    return pl.pallas_call(
        functools.partial(kernel, n_hst, n_dev),
        out_shape=jax.ShapeDtypeStruct(candidate_ids.shape, F32),
        in_specs=[pl.BlockSpec(memory_space=pltpu.HBM)] * len(operands),
        out_specs=pl.BlockSpec(memory_space=pltpu.VMEM),
        scratch_shapes=[
            *[space(a.shape, a.dtype) for space, a in zip(spaces, operands)],
            pltpu.VMEM((n_hst, 1, 128), F32),
            pltpu.VMEM((n_hst, 1, 128), F32),
            pltpu.VMEM((n_hst, 2 * CAP, width // 2), BF16),
            pltpu.VMEM((n_hst, 2 * CAP, width // 2), BF16),
            pltpu.VMEM((2, n_dev, half, width), BF16),
            pltpu.VMEM((collected, 2 * width), BF16),
            dma((len(operands),)),
            dma,
            dma((chunks,)),
            dma,
            dma((chunks,)),
            dma,
            dma,
            dma,
            dma,
        ],
        compiler_params=pltpu.CompilerParams(
            collective_id=0, has_side_effects=True, vmem_limit_bytes=48 * 1024 * 1024
        ),
    )(*[pltpu.with_memory_space_constraint(a, pltpu.HBM) for a in operands])


def solution(mesh):
    rows = P(("hst", "dev"), None)
    placed = (
        P("dev", None),
        rows,
        rows,
        rows,
        P(("hst", "dev")),
        rows,
        rows,
        P(("hst", "dev")),
        P(),
        P(),
        P(),
        P(),
    )
    return jax.shard_map(
        functools.partial(per_device, mesh.shape["hst"], mesh.shape["dev"]),
        mesh=mesh,
        in_specs=placed,
        out_specs=rows,
        check_vma=False,
    )
```
